32 devices in a mesh: blk: 4 (over x, core), grp: 8 (over z, y).
Axes of the slice: x: 2, y: 2, z: 4, core: 2. Of those that a mesh axis runs over, the one named last changes fastest.
Arguments:
- picture_integer_codes: bfloat16 [896, 768], P(('blk', 'grp')), may hold values from -4 to 4
- picture_code_multiplier: float32 [896], P(('blk', 'grp')), may hold values from 0.01 to 0.1
- caption_integer_codes: bfloat16 [896, 768], P(('blk', 'grp')), may hold values from -4 to 4
- caption_code_multiplier: float32 [896], P(('blk', 'grp')), may hold values from 0.01 to 0.1
- sharpness_factor: float32 [1], replicated, may hold values from 5 to 15
- similarity_shift: float32 [1], replicated, may hold values from -6 to -2
Outputs:
- loss: float32 [1], replicated
- image_grad: float32 [896, 768], P(('blk', 'grp'))
- text_grad: float32 [896, 768], P(('blk', 'grp'))
- temp_grad: float32 [1], replicated
- bias_grad: float32 [1], replicated
The draws below stay inside these ranges and needn't reach their ends.
All inputs are finite; a program needn't handle non-finite values.
Results may differ from the reference program's by a relative error of at most 0.0041.
Values may be sent and summed in bfloat16 or wider, within the bound.
A program may use at most 64 MiB of HBM per device.

```python
import math
import jax
import jax.numpy as jnp
from jax import lax

D = 768
R = 28
B = 896
N_GRP = 8


def level_of(stream_key, shape, pieces, least, high):
    gain, own = 1.0, jax.random.fold_in(stream_key, 6)
    for position, blocks in pieces:
        heights = jnp.exp(jax.random.uniform(jax.random.fold_in(own, position), (blocks,), jnp.float32, least / len(pieces), high / len(pieces)))
        gain = gain * jnp.repeat(heights, shape[position] // blocks).reshape([-1 if axis == position else 1 for axis in range(len(shape))])
    return gain


def gaussian(key, dims, deviation, limit, cuts=(), kind=jnp.bfloat16):
    loudness = level_of(key, dims, cuts, -0.22, 0.18) if cuts else 1.0
    values = jax.random.normal(key, dims, jnp.float32) * deviation * loudness
    return jnp.minimum(jnp.maximum(values, -limit), limit).astype(kind)


def setup_inputs(seed: int = 0) -> dict:
    splits = jax.random.split(jax.random.key(seed), 7)
    picture_integer_codes = gaussian(splits[0], (B, D), 1.0, 4.0, ((0, 32),))
    picture_code_multiplier = jnp.clip(jnp.exp(math.log(0.1) - 2.3025851 * jax.random.uniform(splits[1], (B,), jnp.float32) ** level_of(splits[1], (B,), ((0, 32),), -0.2, 0.2)), 0.01, 0.1)
    caption_integer_codes = gaussian(splits[2], (B, D), 1.0, 4.0, ((0, 32),))
    caption_code_multiplier = jnp.clip(jnp.exp(math.log(0.1) - 2.3025851 * jax.random.uniform(splits[3], (B,), jnp.float32) ** level_of(splits[3], (B,), ((0, 32),), -0.2, 0.2)), 0.01, 0.1)
    sharpness_factor = jnp.clip(jax.random.uniform(splits[4], (1,), jnp.float32, 5.0, 15.0), 5.0, 15.0)
    similarity_shift = jnp.clip(jax.random.uniform(splits[5], (1,), jnp.float32, -6.0, -2.0), -6.0, -2.0)
    return {"picture_integer_codes": picture_integer_codes, "picture_code_multiplier": picture_code_multiplier, "caption_integer_codes": caption_integer_codes, "caption_code_multiplier": caption_code_multiplier, "sharpness_factor": sharpness_factor, "similarity_shift": similarity_shift}


def reference(picture_integer_codes, picture_code_multiplier, caption_integer_codes, caption_code_multiplier, sharpness_factor, similarity_shift):
    images = (picture_code_multiplier[:, None] * picture_integer_codes.astype(jnp.float32)).astype(jnp.bfloat16)
    texts = (caption_code_multiplier[:, None] * caption_integer_codes.astype(jnp.float32)).astype(jnp.bfloat16)
    total = images.shape[0]
    block = N_GRP * R
    count = total // block
    sharpness_number = sharpness_factor[0]
    bias_value = similarity_shift[0]
    columns = jnp.arange(total, dtype=jnp.int32)

    def step(carry, index):
        text_acc, sums = carry
        start = (index * block).astype(jnp.int32)
        rows_here = lax.dynamic_slice_in_dim(images, start, block, 0)
        dots = lax.dot_general(rows_here, texts, (((1,), (1,)), ((), ())), preferred_element_type=jnp.float32)
        logits = sharpness_number * dots + bias_value
        rows_index = start + jnp.arange(block, dtype=jnp.int32)
        positive = rows_index[:, None] == columns[None, :]
        slopes = jax.nn.sigmoid(logits) - positive.astype(jnp.float32)
        loss_terms = jnp.where(positive, jax.nn.softplus(-logits), jax.nn.softplus(logits))
        weights = (sharpness_number * slopes).astype(jnp.bfloat16)
        image_part = jnp.dot(weights, texts, preferred_element_type=jnp.float32)
        text_acc = text_acc + lax.dot_general(weights, rows_here, (((0,), (0,)), ((), ())), preferred_element_type=jnp.float32)
        sums = sums + jnp.stack([jnp.sum(loss_terms), jnp.sum(slopes * dots), jnp.sum(slopes)])
        return (text_acc, sums), image_part

    init = (jnp.zeros(texts.shape, jnp.float32), jnp.zeros((3,), jnp.float32))
    (text_grad, sums), parts = lax.scan(step, init, jnp.arange(count, dtype=jnp.int32))
    image_grad = parts.reshape(total, images.shape[1])
    sums = sums / total
    return sums[0:1], image_grad, text_grad, sums[1:2], sums[2:3]
```

```python
import functools
import itertools

import jax
import jax.numpy as jnp
from jax import lax
from jax.experimental import pallas as pl
from jax.experimental.pallas import tpu as pltpu
from jax.sharding import PartitionSpec as P

MESH = pl.DeviceIdType.MESH


def layout(groups, members):
    cores = 2 if groups % 2 == 0 else 1
    sides = 2 if members % 2 == 0 else 1
    return cores, groups // cores, sides, members // sides


def kernel(
    groups,
    members,
    rows,
    pad,
    pic_ref,
    pic_mul_ref,
    cap_ref,
    cap_mul_ref,
    sharp_ref,
    shift_ref,
    loss_ref,
    image_grad_ref,
    text_grad_ref,
    temp_ref,
    bias_ref,
    stage,
    img,
    txt,
    img_part,
    txt_part,
    img_back,
    txt_back,
    near_out,
    near_in,
    far_out,
    far_in,
    img_send,
    img_recv,
    txt_send,
    txt_recv,
    img_back_send,
    img_back_recv,
    txt_back_send,
    txt_back_recv,
    near_send,
    near_recv,
    far_send,
    far_recv,
):
    cores, chips, sides, planes = layout(groups, members)
    b, g = lax.axis_index("blk"), lax.axis_index("grp")
    chip, core = b // cores, b % cores
    z, y = g // sides, g % sides
    offsets = list(itertools.product(range(sides), range(chips), range(cores)))
    n_img, n_txt = planes, len(offsets)

    def plane_peer(index, sign):
        dy, dx, dc = offsets[index]
        y2 = (y + (dy if sign > 0 else sides - dy)) % sides
        x2 = (chip + (dx if sign > 0 else chips - dx)) % chips
        c2 = (core + (dc if sign > 0 else cores - dc)) % cores
        return (x2 * cores + c2, z * sides + y2)

    def column_peer(index, sign):
        z2 = (z + (index if sign > 0 else planes - index)) % planes
        return (b, z2 * sides + y)

    barrier = pltpu.get_barrier_semaphore()
    for k in range(1, n_img):
        pl.semaphore_signal(barrier, inc=1, device_id=column_peer(k, 1), device_id_type=MESH)
    for k in range(1, n_txt):
        pl.semaphore_signal(barrier, inc=1, device_id=plane_peer(k, 1), device_id_type=MESH)

    def decode(codes_ref, mul_ref, slot):
        diagonal = lax.broadcasted_iota(jnp.int32, (rows, rows), 0) == lax.broadcasted_iota(
            jnp.int32, (rows, rows), 1
        )
        across = jnp.broadcast_to(mul_ref[...].reshape(1, rows), (rows, rows))
        scale = jnp.sum(jnp.where(diagonal, across, 0.0), axis=1, keepdims=True)
        stage[...] = jnp.zeros_like(stage)
        stage[0:rows, :] = scale * codes_ref[...].astype(jnp.float32)
        slot[0:pad, :] = stage[...].astype(jnp.bfloat16)

    def block(ref, k):
        return ref.at[pl.ds(k * pad, pad), :]

    decode(pic_ref, pic_mul_ref, img)
    decode(cap_ref, cap_mul_ref, txt)
    pl.semaphore_wait(barrier, n_img - 1 + n_txt - 1)

    copies = []

    def send(src, dst, send_sem, recv_sem, peer):
        copy = pltpu.make_async_remote_copy(
            src_ref=src,
            dst_ref=dst,
            send_sem=send_sem,
            recv_sem=recv_sem,
            device_id=peer,
            device_id_type=MESH,
        )
        copy.start()
        copies.append(copy)
        return copy

    gathers = []
    for k in range(max(n_img, n_txt) - 1, 0, -1):
        if k < n_txt:
            gathers.append(
                send(block(txt, 0), block(txt, k), txt_send.at[k], txt_recv.at[k], plane_peer(k, 1))
            )
        if k < n_img:
            gathers.append(
                send(block(img, 0), block(img, k), img_send.at[k], img_recv.at[k], column_peer(k, 1))
            )
    for copy in gathers:
        copy.wait_recv()

    sharp = sharp_ref[0]
    shift = shift_ref[0]
    images, texts = img[...], txt[...]
    dots = lax.dot_general(
        images, texts, (((1,), (1,)), ((), ())), preferred_element_type=jnp.float32
    )
    logits = sharp * dots + shift
    row = lax.broadcasted_iota(jnp.int32, dots.shape, 0)
    col = lax.broadcasted_iota(jnp.int32, dots.shape, 1)
    positive = (row == col) & (row < pad)
    real = (row % pad < rows) & (col % pad < rows)
    small = jnp.exp(-jnp.abs(logits))
    below = 1.0 / (1.0 + small)
    slopes = jnp.where(logits >= 0, below, small * below) - jnp.where(positive, 1.0, 0.0)
    terms = jnp.maximum(jnp.where(positive, -logits, logits), 0.0) + jnp.log1p(small)
    weights = (sharp * slopes).astype(jnp.bfloat16)

    def total(x):
        return jnp.sum(jnp.sum(x, axis=0, keepdims=True), axis=1, keepdims=True)

    lane = lax.broadcasted_iota(jnp.int32, near_out.shape, 0)
    near = jnp.where(
        lane == 0,
        total(jnp.where(real, terms, 0.0)),
        jnp.where(lane == 1, total(slopes * dots), total(jnp.where(real, slopes, 0.0))),
    )
    near_out[...] = near
    nears = [
        send(near_out, near_in.at[k], near_send.at[k], near_recv.at[k], plane_peer(k, 1))
        for k in range(1, n_txt)
    ]

    txt_total = lax.dot_general(
        weights, images, (((0,), (0,)), ((), ())), preferred_element_type=jnp.float32
    )
    txt_part[...] = txt_total.astype(jnp.bfloat16)
    txt_backs = [
        send(
            block(txt_part, k),
            txt_back.at[k],
            txt_back_send.at[k],
            txt_back_recv.at[k],
            plane_peer(k, -1),
        )
        for k in range(n_txt - 1, 0, -1)
    ]
    img_total = jnp.dot(weights, texts, preferred_element_type=jnp.float32)
    img_part[...] = img_total.astype(jnp.bfloat16)
    img_backs = [
        send(
            block(img_part, k),
            img_back.at[k],
            img_back_send.at[k],
            img_back_recv.at[k],
            column_peer(k, -1),
        )
        for k in range(n_img - 1, 0, -1)
    ]

    for k, copy in enumerate(nears, 1):
        copy.wait_recv()
        near = near + near_in[k]
    far_out[...] = near
    fars = [
        send(far_out, far_in.at[k], far_send.at[k], far_recv.at[k], column_peer(k, 1))
        for k in range(1, n_img)
    ]

    own = txt_total[0:pad]
    for k, copy in zip(range(n_txt - 1, 0, -1), txt_backs):
        copy.wait_recv()
        own = own + txt_back[k].astype(jnp.float32)
    text_grad_ref[...] = own[0:rows]
    own = img_total[0:pad]
    for k, copy in zip(range(n_img - 1, 0, -1), img_backs):
        copy.wait_recv()
        own = own + img_back[k].astype(jnp.float32)
    image_grad_ref[...] = own[0:rows]

    for k, copy in enumerate(fars, 1):
        copy.wait_recv()
        near = near + far_in[k]
    near = near / (rows * groups * members)
    loss_ref[0] = near[0, 0]
    temp_ref[0] = near[1, 0]
    bias_ref[0] = near[2, 0]
    for copy in copies:
        copy.wait_send()


def body(groups, members, pic, pic_mul, cap, cap_mul, sharp, shift):
    rows, width = pic.shape
    pad = -(-rows // 16) * 16
    cores, chips, sides, planes = layout(groups, members)
    n_img, n_txt = planes, sides * chips * cores
    vmem = pl.BlockSpec(memory_space=pltpu.VMEM)
    smem = pl.BlockSpec(memory_space=pltpu.SMEM)
    one = jax.ShapeDtypeStruct((1,), jnp.float32)
    grad = jax.ShapeDtypeStruct((rows, width), jnp.float32)
    bf16, f32, dma = jnp.bfloat16, jnp.float32, pltpu.SemaphoreType.DMA
    return pl.pallas_call(
        functools.partial(kernel, groups, members, rows, pad),
        out_shape=(one, grad, grad, one, one),
        in_specs=[vmem, vmem, vmem, vmem, smem, smem],
        out_specs=(smem, vmem, vmem, smem, smem),
        scratch_shapes=[
            pltpu.VMEM((pad, width), f32),
            pltpu.VMEM((n_img * pad, width), bf16),
            pltpu.VMEM((n_txt * pad, width), bf16),
            pltpu.VMEM((n_img * pad, width), bf16),
            pltpu.VMEM((n_txt * pad, width), bf16),
            pltpu.VMEM((n_img, pad, width), bf16),
            pltpu.VMEM((n_txt, pad, width), bf16),
            pltpu.VMEM((8, 128), f32),
            pltpu.VMEM((n_txt, 8, 128), f32),
            pltpu.VMEM((8, 128), f32),
            pltpu.VMEM((n_img, 8, 128), f32),
            dma((n_img,)),
            dma((n_img,)),
            dma((n_txt,)),
            dma((n_txt,)),
            dma((n_img,)),
            dma((n_img,)),
            dma((n_txt,)),
            dma((n_txt,)),
            dma((n_txt,)),
            dma((n_txt,)),
            dma((n_img,)),
            dma((n_img,)),
        ],
        compiler_params=pltpu.CompilerParams(
            collective_id=0, has_side_effects=True, vmem_limit_bytes=32 * 1024 * 1024
        ),
    )(pic, pic_mul, cap, cap_mul, sharp, shift)


def solution(mesh):
    placed = (
        P(("blk", "grp"), None),
        P(("blk", "grp")),
        P(("blk", "grp"), None),
        P(("blk", "grp")),
        P(),
        P(),
    )
    return jax.shard_map(
        functools.partial(body, mesh.shape["blk"], mesh.shape["grp"]),
        mesh=mesh,
        in_specs=placed,
        out_specs=(P(), P(("blk", "grp"), None), P(("blk", "grp"), None), P(), P()),
        check_vma=False,
    )
```

```python
import functools
import itertools

import jax
import jax.numpy as jnp
from jax import lax
from jax.experimental import pallas as pl
from jax.experimental.pallas import tpu as pltpu
from jax.sharding import PartitionSpec as P

MESH = pl.DeviceIdType.MESH


def layout(groups, members):
    cores = 2 if groups % 2 == 0 else 1
    sides = 2 if members % 2 == 0 else 1
    return cores, groups // cores, sides, members // sides


def kernel(
    groups,
    members,
    rows,
    pad,
    pic_hbm,
    pic_mul_hbm,
    cap_hbm,
    cap_mul_hbm,
    sharp_hbm,
    shift_hbm,
    image_grad_ref,
    text_grad_ref,
    sums_ref,
    pic_ref,
    pic_mul_ref,
    cap_ref,
    cap_mul_ref,
    sharp_ref,
    shift_ref,
    load_sem,
    stage,
    img,
    txt,
    img_part,
    txt_part,
    img_back,
    txt_back,
    near_out,
    near_in,
    far_out,
    far_in,
    img_send,
    img_recv,
    txt_send,
    txt_recv,
    img_back_send,
    img_back_recv,
    txt_back_send,
    txt_back_recv,
    near_send,
    near_recv,
    far_send,
    far_recv,
):
    cores, chips, sides, planes = layout(groups, members)
    b, g = lax.axis_index("blk"), lax.axis_index("grp")
    chip, core = b // cores, b % cores
    z, y = g // sides, g % sides
    offsets = list(itertools.product(range(sides), range(chips), range(cores)))
    n_img, n_txt = planes, len(offsets)

    def plane_peer(index, sign):
        dy, dx, dc = offsets[index]
        y2 = (y + (dy if sign > 0 else sides - dy)) % sides
        x2 = (chip + (dx if sign > 0 else chips - dx)) % chips
        c2 = (core + (dc if sign > 0 else cores - dc)) % cores
        return (x2 * cores + c2, z * sides + y2)

    def column_peer(index, sign):
        z2 = (z + (index if sign > 0 else planes - index)) % planes
        return (b, z2 * sides + y)

    loads = [
        pltpu.make_async_copy(src, dst, load_sem.at[i])
        for i, (src, dst) in enumerate(
            [
                (pic_mul_hbm, pic_mul_ref),
                (pic_hbm, pic_ref),
                (cap_mul_hbm, cap_mul_ref),
                (cap_hbm, cap_ref),
                (sharp_hbm, sharp_ref),
                (shift_hbm, shift_ref),
            ]
        )
    ]
    for load in loads:
        load.start()
    barrier = pltpu.get_barrier_semaphore()
    for k in range(1, n_img):
        pl.semaphore_signal(barrier, inc=1, device_id=column_peer(k, 1), device_id_type=MESH)
    for k in range(1, n_txt):
        pl.semaphore_signal(barrier, inc=1, device_id=plane_peer(k, 1), device_id_type=MESH)

    def decode(codes_ref, mul_ref, slot):
        diagonal = lax.broadcasted_iota(jnp.int32, (rows, rows), 0) == lax.broadcasted_iota(
            jnp.int32, (rows, rows), 1
        )
        across = jnp.broadcast_to(mul_ref[...].reshape(1, rows), (rows, rows))
        scale = jnp.sum(jnp.where(diagonal, across, 0.0), axis=1, keepdims=True)
        stage[...] = jnp.zeros_like(stage)
        stage[0:rows, :] = scale * codes_ref[...].astype(jnp.float32)
        slot[0:pad, :] = stage[...].astype(jnp.bfloat16)

    def block(ref, k):
        return ref.at[pl.ds(k * pad, pad), :]

    loads[0].wait()
    loads[1].wait()
    decode(pic_ref, pic_mul_ref, img)
    pl.semaphore_wait(barrier, n_img - 1 + n_txt - 1)

    copies = []

    def send(src, dst, send_sem, recv_sem, peer):
        copy = pltpu.make_async_remote_copy(
            src_ref=src,
            dst_ref=dst,
            send_sem=send_sem,
            recv_sem=recv_sem,
            device_id=peer,
            device_id_type=MESH,
        )
        copy.start()
        copies.append(copy)
        return copy

    gathers = [
        send(block(img, 0), block(img, k), img_send.at[k], img_recv.at[k], column_peer(k, 1))
        for k in range(n_img - 1, 0, -1)
    ]
    loads[2].wait()
    loads[3].wait()
    decode(cap_ref, cap_mul_ref, txt)
    gathers += [
        send(block(txt, 0), block(txt, k), txt_send.at[k], txt_recv.at[k], plane_peer(k, 1))
        for k in range(n_txt - 1, 0, -1)
    ]
    loads[4].wait()
    loads[5].wait()
    for copy in gathers:
        copy.wait_recv()

    sharp = sharp_ref[0]
    shift = shift_ref[0]
    images, texts = img[...], txt[...]
    dots = lax.dot_general(
        images, texts, (((1,), (1,)), ((), ())), preferred_element_type=jnp.float32
    )
    logits = sharp * dots + shift
    row = lax.broadcasted_iota(jnp.int32, dots.shape, 0)
    col = lax.broadcasted_iota(jnp.int32, dots.shape, 1)
    positive = (row == col) & (row < pad)
    real = (row % pad < rows) & (col % pad < rows)
    small = jnp.exp(-jnp.abs(logits))
    below = 1.0 / (1.0 + small)
    slopes = jnp.where(logits >= 0, below, small * below) - jnp.where(positive, 1.0, 0.0)
    terms = jnp.maximum(jnp.where(positive, -logits, logits), 0.0) + jnp.log1p(small)
    weights = (sharp * slopes).astype(jnp.bfloat16)

    def total(x):
        return jnp.sum(jnp.sum(x, axis=0, keepdims=True), axis=1, keepdims=True)

    lane = lax.broadcasted_iota(jnp.int32, near_out.shape, 0)
    near = jnp.where(
        lane == 0,
        total(jnp.where(real, terms, 0.0)),
        jnp.where(lane == 1, total(slopes * dots), total(jnp.where(real, slopes, 0.0))),
    )
    near_out[...] = near
    nears = [
        send(near_out, near_in.at[k], near_send.at[k], near_recv.at[k], plane_peer(k, 1))
        for k in range(1, n_txt)
    ]

    txt_total = lax.dot_general(
        weights, images, (((0,), (0,)), ((), ())), preferred_element_type=jnp.float32
    )
    txt_part[...] = txt_total.astype(jnp.bfloat16)
    txt_backs = [
        send(
            block(txt_part, k),
            txt_back.at[k],
            txt_back_send.at[k],
            txt_back_recv.at[k],
            plane_peer(k, -1),
        )
        for k in range(n_txt - 1, 0, -1)
    ]
    img_total = jnp.dot(weights, texts, preferred_element_type=jnp.float32)
    img_part[...] = img_total.astype(jnp.bfloat16)
    img_backs = [
        send(
            block(img_part, k),
            img_back.at[k],
            img_back_send.at[k],
            img_back_recv.at[k],
            column_peer(k, -1),
        )
        for k in range(n_img - 1, 0, -1)
    ]

    for k, copy in enumerate(nears, 1):
        copy.wait_recv()
        near = near + near_in[k]
    far_out[...] = near
    fars = [
        send(far_out, far_in.at[k], far_send.at[k], far_recv.at[k], column_peer(k, 1))
        for k in range(1, n_img)
    ]

    own = txt_total[0:pad]
    for k, copy in zip(range(n_txt - 1, 0, -1), txt_backs):
        copy.wait_recv()
        own = own + txt_back[k].astype(jnp.float32)
    text_grad_ref[...] = own[0:rows]
    own = img_total[0:pad]
    for k, copy in zip(range(n_img - 1, 0, -1), img_backs):
        copy.wait_recv()
        own = own + img_back[k].astype(jnp.float32)
    image_grad_ref[...] = own[0:rows]

    for k, copy in enumerate(fars, 1):
        copy.wait_recv()
        near = near + far_in[k]
    sums_ref[...] = near / (rows * groups * members)
    for copy in copies:
        copy.wait_send()


def deliver(image_ref, text_ref, sums_ref, loss_ref, image_out, text_out, temp_ref, bias_ref, sem):
    copies = [
        pltpu.make_async_copy(src, dst, sem.at[i])
        for i, (src, dst) in enumerate([(image_ref, image_out), (text_ref, text_out)])
    ]
    for copy in copies:
        copy.start()
    sums = sums_ref[...]
    loss_ref[0] = sums[0, 0]
    temp_ref[0] = sums[1, 0]
    bias_ref[0] = sums[2, 0]
    for copy in copies:
        copy.wait()


def body(groups, members, pic, pic_mul, cap, cap_mul, sharp, shift):
    rows, width = pic.shape
    pad = -(-rows // 16) * 16
    cores, chips, sides, planes = layout(groups, members)
    n_img, n_txt = planes, sides * chips * cores
    vmem = pl.BlockSpec(memory_space=pltpu.VMEM)
    smem = pl.BlockSpec(memory_space=pltpu.SMEM)
    hbm = pl.BlockSpec(memory_space=pltpu.HBM)
    bf16, f32, dma = jnp.bfloat16, jnp.float32, pltpu.SemaphoreType.DMA
    one = jax.ShapeDtypeStruct((1,), f32)
    grad = jax.ShapeDtypeStruct((rows, width), f32)
    tile = jax.ShapeDtypeStruct((8, 128), f32)
    image_grad, text_grad, sums = pl.pallas_call(
        functools.partial(kernel, groups, members, rows, pad),
        out_shape=(grad, grad, tile),
        in_specs=[hbm] * 6,
        out_specs=(vmem, vmem, vmem),
        scratch_shapes=[
            pltpu.VMEM((rows, width), bf16),
            pltpu.VMEM((rows,), f32),
            pltpu.VMEM((rows, width), bf16),
            pltpu.VMEM((rows,), f32),
            pltpu.SMEM((1,), f32),
            pltpu.SMEM((1,), f32),
            dma((6,)),
            pltpu.VMEM((pad, width), f32),
            pltpu.VMEM((n_img * pad, width), bf16),
            pltpu.VMEM((n_txt * pad, width), bf16),
            pltpu.VMEM((n_img * pad, width), bf16),
            pltpu.VMEM((n_txt * pad, width), bf16),
            pltpu.VMEM((n_img, pad, width), bf16),
            pltpu.VMEM((n_txt, pad, width), bf16),
            pltpu.VMEM((8, 128), f32),
            pltpu.VMEM((n_txt, 8, 128), f32),
            pltpu.VMEM((8, 128), f32),
            pltpu.VMEM((n_img, 8, 128), f32),
            dma((n_img,)),
            dma((n_img,)),
            dma((n_txt,)),
            dma((n_txt,)),
            dma((n_img,)),
            dma((n_img,)),
            dma((n_txt,)),
            dma((n_txt,)),
            dma((n_txt,)),
            dma((n_txt,)),
            dma((n_img,)),
            dma((n_img,)),
        ],
        compiler_params=pltpu.CompilerParams(
            collective_id=0, has_side_effects=True, vmem_limit_bytes=64 * 1024 * 1024
        ),
    )(pic, pic_mul, cap, cap_mul, sharp, shift)
    return pl.pallas_call(
        deliver,
        out_shape=(one, grad, grad, one, one),
        in_specs=[vmem] * 3,
        out_specs=(smem, hbm, hbm, smem, smem),
        scratch_shapes=[dma((2,))],
    )(image_grad, text_grad, sums)


def solution(mesh):
    placed = (
        P(("blk", "grp"), None),
        P(("blk", "grp")),
        P(("blk", "grp"), None),
        P(("blk", "grp")),
        P(),
        P(),
    )
    return jax.shard_map(
        functools.partial(body, mesh.shape["blk"], mesh.shape["grp"]),
        mesh=mesh,
        in_specs=placed,
        out_specs=(P(), P(("blk", "grp"), None), P(("blk", "grp"), None), P(), P()),
        check_vma=False,
    )
```

```python
import functools
import itertools

import jax
import jax.numpy as jnp
from jax import lax
from jax.experimental import pallas as pl
from jax.experimental.pallas import tpu as pltpu
from jax.sharding import PartitionSpec as P

MESH = pl.DeviceIdType.MESH


def layout(groups, members):
    cores = 2 if groups % 2 == 0 else 1
    sides = 2 if members % 2 == 0 else 1
    return cores, groups // cores, sides, members // sides


def kernel(
    groups,
    members,
    rows,
    pad,
    pic_hbm,
    pic_mul_hbm,
    cap_hbm,
    cap_mul_hbm,
    sharp_hbm,
    shift_hbm,
    image_grad_ref,
    text_grad_ref,
    sums_ref,
    pic_ref,
    pic_mul_ref,
    cap_ref,
    cap_mul_ref,
    sharp_ref,
    shift_ref,
    load_sem,
    stage,
    img,
    txt,
    img_part,
    txt_part,
    img_back,
    txt_back,
    near_out,
    near_in,
    far_out,
    far_in,
    img_send,
    img_recv,
    txt_send,
    txt_recv,
    img_back_send,
    img_back_recv,
    txt_back_send,
    txt_back_recv,
    near_send,
    near_recv,
    far_send,
    far_recv,
):
    cores, chips, sides, planes = layout(groups, members)
    b, g = lax.axis_index("blk"), lax.axis_index("grp")
    chip, core = b // cores, b % cores
    z, y = g // sides, g % sides
    offsets = list(itertools.product(range(sides), range(chips), range(cores)))
    n_img, n_txt = planes, len(offsets)

    def plane_peer(index, sign):
        dy, dx, dc = offsets[index]
        y2 = (y + (dy if sign > 0 else sides - dy)) % sides
        x2 = (chip + (dx if sign > 0 else chips - dx)) % chips
        c2 = (core + (dc if sign > 0 else cores - dc)) % cores
        return (x2 * cores + c2, z * sides + y2)

    def column_peer(index, sign):
        z2 = (z + (index if sign > 0 else planes - index)) % planes
        return (b, z2 * sides + y)

    loads = [
        pltpu.make_async_copy(src, dst, load_sem.at[i])
        for i, (src, dst) in enumerate(
            [
                (pic_mul_hbm, pic_mul_ref),
                (pic_hbm, pic_ref),
                (cap_mul_hbm, cap_mul_ref),
                (cap_hbm, cap_ref),
                (sharp_hbm, sharp_ref),
                (shift_hbm, shift_ref),
            ]
        )
    ]
    for load in loads:
        load.start()
    barrier = pltpu.get_barrier_semaphore()
    for k in range(1, n_img):
        pl.semaphore_signal(barrier, inc=1, device_id=column_peer(k, 1), device_id_type=MESH)
    for k in range(1, n_txt):
        pl.semaphore_signal(barrier, inc=1, device_id=plane_peer(k, 1), device_id_type=MESH)

    def decode(codes_ref, mul_ref, slot):
        diagonal = lax.broadcasted_iota(jnp.int32, (rows, rows), 0) == lax.broadcasted_iota(
            jnp.int32, (rows, rows), 1
        )
        across = jnp.broadcast_to(mul_ref[...].reshape(1, rows), (rows, rows))
        scale = jnp.sum(jnp.where(diagonal, across, 0.0), axis=1, keepdims=True)
        stage[...] = jnp.zeros_like(stage)
        stage[0:rows, :] = scale * codes_ref[...].astype(jnp.float32)
        slot[0:pad, :] = stage[...].astype(jnp.bfloat16)

    def block(ref, k):
        return ref.at[pl.ds(k * pad, pad), :]

    loads[0].wait()
    loads[1].wait()
    decode(pic_ref, pic_mul_ref, img)
    pl.semaphore_wait(barrier, n_img - 1 + n_txt - 1)

    copies = []

    def send(src, dst, send_sem, recv_sem, peer):
        copy = pltpu.make_async_remote_copy(
            src_ref=src,
            dst_ref=dst,
            send_sem=send_sem,
            recv_sem=recv_sem,
            device_id=peer,
            device_id_type=MESH,
        )
        copy.start()
        copies.append(copy)
        return copy

    gathers = [
        send(block(img, 0), block(img, k), img_send.at[k], img_recv.at[k], column_peer(k, 1))
        for k in range(n_img - 1, 0, -1)
    ]
    loads[2].wait()
    loads[3].wait()
    decode(cap_ref, cap_mul_ref, txt)
    gathers += [
        send(block(txt, 0), block(txt, k), txt_send.at[k], txt_recv.at[k], plane_peer(k, 1))
        for k in range(n_txt - 1, 0, -1)
    ]
    loads[4].wait()
    loads[5].wait()
    for copy in gathers:
        copy.wait_recv()

    sharp = sharp_ref[0]
    shift = shift_ref[0]
    images, texts = img[...], txt[...]
    dots = lax.dot_general(
        images, texts, (((1,), (1,)), ((), ())), preferred_element_type=jnp.float32
    )
    logits = sharp * dots + shift
    row = lax.broadcasted_iota(jnp.int32, dots.shape, 0)
    col = lax.broadcasted_iota(jnp.int32, dots.shape, 1)
    positive = (row == col) & (row < pad)
    real = (row % pad < rows) & (col % pad < rows)
    small = jnp.exp(-jnp.abs(logits))
    below = 1.0 / (1.0 + small)
    slopes = jnp.where(logits >= 0, below, small * below) - jnp.where(positive, 1.0, 0.0)
    terms = jnp.maximum(jnp.where(positive, -logits, logits), 0.0) + jnp.log1p(small)
    weights = (sharp * slopes).astype(jnp.bfloat16)

    def total(x):
        return jnp.sum(jnp.sum(x, axis=0, keepdims=True), axis=1, keepdims=True)

    lane = lax.broadcasted_iota(jnp.int32, near_out.shape, 0)
    near = jnp.where(
        lane == 0,
        total(jnp.where(real, terms, 0.0)),
        jnp.where(lane == 1, total(slopes * dots), total(jnp.where(real, slopes, 0.0))),
    )
    near_out[...] = near
    nears = [
        send(near_out, near_in.at[k], near_send.at[k], near_recv.at[k], plane_peer(k, 1))
        for k in range(1, n_txt)
    ]

    txt_total = lax.dot_general(
        weights, images, (((0,), (0,)), ((), ())), preferred_element_type=jnp.float32
    )
    txt_part[...] = txt_total.astype(jnp.bfloat16)
    txt_backs = [
        send(
            block(txt_part, k),
            txt_back.at[k],
            txt_back_send.at[k],
            txt_back_recv.at[k],
            plane_peer(k, -1),
        )
        for k in range(n_txt - 1, 0, -1)
    ]
    img_total = jnp.dot(weights, texts, preferred_element_type=jnp.float32)
    img_part[...] = img_total.astype(jnp.bfloat16)
    img_backs = [
        send(
            block(img_part, k),
            img_back.at[k],
            img_back_send.at[k],
            img_back_recv.at[k],
            column_peer(k, -1),
        )
        for k in range(n_img - 1, 0, -1)
    ]

    for k, copy in enumerate(nears, 1):
        copy.wait_recv()
        near = near + near_in[k]
    far_out[...] = near
    fars = [
        send(far_out, far_in.at[k], far_send.at[k], far_recv.at[k], column_peer(k, 1))
        for k in range(1, n_img)
    ]

    own = txt_total[0:pad]
    for k, copy in zip(range(n_txt - 1, 0, -1), txt_backs):
        copy.wait_recv()
        own = own + txt_back[k].astype(jnp.float32)
    text_grad_ref[...] = own[0:rows]
    own = img_total[0:pad]
    for k, copy in zip(range(n_img - 1, 0, -1), img_backs):
        copy.wait_recv()
        own = own + img_back[k].astype(jnp.float32)
    image_grad_ref[...] = own[0:rows]

    for k, copy in enumerate(fars, 1):
        copy.wait_recv()
        near = near + far_in[k]
    sums_ref[...] = near / (rows * groups * members)
    for copy in copies:
        copy.wait_send()


def deliver(image_ref, text_ref, sums_ref, loss_ref, image_out, text_out, temp_ref, bias_ref, sem):
    copies = [
        pltpu.make_async_copy(src, dst, sem.at[i])
        for i, (src, dst) in enumerate([(image_ref, image_out), (text_ref, text_out)])
    ]
    for copy in copies:
        copy.start()
    sums = sums_ref[...]
    loss_ref[0] = sums[0, 0]
    temp_ref[0] = sums[1, 0]
    bias_ref[0] = sums[2, 0]
    for copy in copies:
        copy.wait()


def body(groups, members, pic, pic_mul, cap, cap_mul, sharp, shift):
    rows, width = pic.shape
    pad = -(-rows // 16) * 16
    cores, chips, sides, planes = layout(groups, members)
    n_img, n_txt = planes, sides * chips * cores
    vmem = pl.BlockSpec(memory_space=pltpu.VMEM)
    smem = pl.BlockSpec(memory_space=pltpu.SMEM)
    hbm = pl.BlockSpec(memory_space=pltpu.HBM)
    bf16, f32, dma = jnp.bfloat16, jnp.float32, pltpu.SemaphoreType.DMA
    one = jax.ShapeDtypeStruct((1,), f32)
    grad = jax.ShapeDtypeStruct((rows, width), f32)
    tile = jax.ShapeDtypeStruct((8, 128), f32)
    image_grad, text_grad, sums = pl.pallas_call(
        functools.partial(kernel, groups, members, rows, pad),
        out_shape=(pltpu.VMEM((rows, width), f32), pltpu.VMEM((rows, width), f32), pltpu.VMEM((8, 128), f32)),
        in_specs=[hbm] * 6,
        out_specs=(vmem, vmem, vmem),
        scratch_shapes=[
            pltpu.VMEM((rows, width), bf16),
            pltpu.VMEM((rows,), f32),
            pltpu.VMEM((rows, width), bf16),
            pltpu.VMEM((rows,), f32),
            pltpu.SMEM((1,), f32),
            pltpu.SMEM((1,), f32),
            dma((6,)),
            pltpu.VMEM((pad, width), f32),
            pltpu.VMEM((n_img * pad, width), bf16),
            pltpu.VMEM((n_txt * pad, width), bf16),
            pltpu.VMEM((n_img * pad, width), bf16),
            pltpu.VMEM((n_txt * pad, width), bf16),
            pltpu.VMEM((n_img, pad, width), bf16),
            pltpu.VMEM((n_txt, pad, width), bf16),
            pltpu.VMEM((8, 128), f32),
            pltpu.VMEM((n_txt, 8, 128), f32),
            pltpu.VMEM((8, 128), f32),
            pltpu.VMEM((n_img, 8, 128), f32),
            dma((n_img,)),
            dma((n_img,)),
            dma((n_txt,)),
            dma((n_txt,)),
            dma((n_img,)),
            dma((n_img,)),
            dma((n_txt,)),
            dma((n_txt,)),
            dma((n_txt,)),
            dma((n_txt,)),
            dma((n_img,)),
            dma((n_img,)),
        ],
        compiler_params=pltpu.CompilerParams(
            collective_id=0, has_side_effects=True, vmem_limit_bytes=63 * 1024 * 1024
        ),
    )(pic, pic_mul, cap, cap_mul, sharp, shift)
    return pl.pallas_call(
        deliver,
        out_shape=(one, grad, grad, one, one),
        in_specs=[vmem] * 3,
        out_specs=(smem, hbm, hbm, smem, smem),
        scratch_shapes=[dma((2,))],
        compiler_params=pltpu.CompilerParams(vmem_limit_bytes=4 * 1024 * 1024),
    )(image_grad, text_grad, sums)


def solution(mesh):
    placed = (
        P(("blk", "grp"), None),
        P(("blk", "grp")),
        P(("blk", "grp"), None),
        P(("blk", "grp")),
        P(),
        P(),
    )
    return jax.shard_map(
        functools.partial(body, mesh.shape["blk"], mesh.shape["grp"]),
        mesh=mesh,
        in_specs=placed,
        out_specs=(P(), P(("blk", "grp"), None), P(("blk", "grp"), None), P(), P()),
        check_vma=False,
    )
```

```python
import functools
import itertools

import jax
import jax.numpy as jnp
from jax import lax
from jax.experimental import pallas as pl
from jax.experimental.pallas import tpu as pltpu
from jax.sharding import PartitionSpec as P

MESH = pl.DeviceIdType.MESH


def layout(groups, members):
    cores = 2 if groups % 2 == 0 else 1
    sides = 2 if members % 2 == 0 else 1
    return cores, groups // cores, sides, members // sides


def kernel(
    groups,
    members,
    rows,
    pad,
    pic_hbm,
    pic_mul_hbm,
    cap_hbm,
    cap_mul_hbm,
    sharp_hbm,
    shift_hbm,
    image_grad_ref,
    text_grad_ref,
    sums_ref,
    pic_ref,
    pic_mul_ref,
    cap_ref,
    cap_mul_ref,
    sharp_ref,
    shift_ref,
    load_sem,
    stage,
    img,
    txt,
    img_part,
    txt_part,
    img_back,
    txt_back,
    near_out,
    near_in,
    far_out,
    far_in,
    img_send,
    img_recv,
    txt_send,
    txt_recv,
    img_back_send,
    img_back_recv,
    txt_back_send,
    txt_back_recv,
    near_send,
    near_recv,
    far_send,
    far_recv,
):
    cores, chips, sides, planes = layout(groups, members)
    b, g = lax.axis_index("blk"), lax.axis_index("grp")
    chip, core = b // cores, b % cores
    z, y = g // sides, g % sides
    offsets = list(itertools.product(range(sides), range(chips), range(cores)))
    n_img, n_txt = planes, len(offsets)

    def plane_peer(index, sign):
        dy, dx, dc = offsets[index]
        y2 = (y + (dy if sign > 0 else sides - dy)) % sides
        x2 = (chip + (dx if sign > 0 else chips - dx)) % chips
        c2 = (core + (dc if sign > 0 else cores - dc)) % cores
        return (x2 * cores + c2, z * sides + y2)

    def column_peer(index, sign):
        z2 = (z + (index if sign > 0 else planes - index)) % planes
        return (b, z2 * sides + y)

    barrier = pltpu.get_barrier_semaphore()
    for k in range(n_img - 1, 0, -1):
        pl.semaphore_signal(barrier, inc=1, device_id=column_peer(k, 1), device_id_type=MESH)
    for k in range(n_txt - 1, 0, -1):
        pl.semaphore_signal(barrier, inc=1, device_id=plane_peer(k, 1), device_id_type=MESH)

    loads = [
        pltpu.make_async_copy(src, dst, load_sem.at[i])
        for i, (src, dst) in enumerate(
            [
                (pic_mul_hbm, pic_mul_ref),
                (pic_hbm, pic_ref),
                (cap_mul_hbm, cap_mul_ref),
                (cap_hbm, cap_ref),
                (sharp_hbm, sharp_ref),
                (shift_hbm, shift_ref),
            ]
        )
    ]
    for load in loads:
        load.start()
    def decode(codes_ref, mul_ref, slot):
        diagonal = lax.broadcasted_iota(jnp.int32, (rows, rows), 0) == lax.broadcasted_iota(
            jnp.int32, (rows, rows), 1
        )
        across = jnp.broadcast_to(mul_ref[...].reshape(1, rows), (rows, rows))
        scale = jnp.sum(jnp.where(diagonal, across, 0.0), axis=1, keepdims=True)
        stage[0:rows, :] = scale * codes_ref[...].astype(jnp.float32)
        slot[0:pad, :] = stage[...].astype(jnp.bfloat16)

    def block(ref, k):
        return ref.at[pl.ds(k * pad, pad), :]

    stage[...] = jnp.zeros_like(stage)
    loads[0].wait()
    loads[1].wait()
    decode(pic_ref, pic_mul_ref, img)
    pl.semaphore_wait(barrier, n_img - 1 + n_txt - 1)

    copies = []

    def send(src, dst, send_sem, recv_sem, peer):
        copy = pltpu.make_async_remote_copy(
            src_ref=src,
            dst_ref=dst,
            send_sem=send_sem,
            recv_sem=recv_sem,
            device_id=peer,
            device_id_type=MESH,
        )
        copy.start()
        copies.append(copy)
        return copy

    gathers = [
        send(block(img, 0), block(img, k), img_send.at[k], img_recv.at[k], column_peer(k, 1))
        for k in range(n_img - 1, 0, -1)
    ]
    loads[2].wait()
    loads[3].wait()
    decode(cap_ref, cap_mul_ref, txt)
    gathers += [
        send(block(txt, 0), block(txt, k), txt_send.at[k], txt_recv.at[k], plane_peer(k, 1))
        for k in range(n_txt - 1, 0, -1)
    ]
    loads[4].wait()
    loads[5].wait()
    for copy in gathers:
        copy.wait_recv()

    sharp = sharp_ref[0]
    shift = shift_ref[0]
    images, texts = img[...], txt[...]
    dots = lax.dot_general(
        images, texts, (((1,), (1,)), ((), ())), preferred_element_type=jnp.float32
    )
    logits = sharp * dots + shift
    row = lax.broadcasted_iota(jnp.int32, dots.shape, 0)
    col = lax.broadcasted_iota(jnp.int32, dots.shape, 1)
    positive = (row == col) & (row < pad)
    real = (row % pad < rows) & (col % pad < rows)
    small = jnp.exp(-jnp.abs(logits))
    below = 1.0 / (1.0 + small)
    slopes = jnp.where(logits >= 0, below, small * below) - jnp.where(positive, 1.0, 0.0)
    terms = jnp.maximum(jnp.where(positive, -logits, logits), 0.0) + jnp.log1p(small)
    weights = (sharp * slopes).astype(jnp.bfloat16)

    def total(x):
        return jnp.sum(jnp.sum(x, axis=0, keepdims=True), axis=1, keepdims=True)

    lane = lax.broadcasted_iota(jnp.int32, near_out.shape, 0)
    near = jnp.where(
        lane == 0,
        total(jnp.where(real, terms, 0.0)),
        jnp.where(lane == 1, total(slopes * dots), total(jnp.where(real, slopes, 0.0))),
    )
    near_out[...] = near
    nears = [
        send(near_out, near_in.at[k], near_send.at[k], near_recv.at[k], plane_peer(k, 1))
        for k in range(1, n_txt)
    ]

    txt_backs = []
    half = (n_txt // 2) * pad
    for low, high in ((half, n_txt * pad), (0, half)):
        txt_total = lax.dot_general(
            weights[:, low:high], images, (((0,), (0,)), ((), ())), preferred_element_type=jnp.float32
        )
        txt_part[low:high, :] = txt_total.astype(jnp.bfloat16)
        for k in range(high // pad - 1, max(low // pad, 1) - 1, -1):
            txt_backs.append(
                send(
                    block(txt_part, k),
                    txt_back.at[k],
                    txt_back_send.at[k],
                    txt_back_recv.at[k],
                    plane_peer(k, -1),
                )
            )
    img_total = jnp.dot(weights, texts, preferred_element_type=jnp.float32)
    img_part[...] = img_total.astype(jnp.bfloat16)
    img_backs = [
        send(
            block(img_part, k),
            img_back.at[k],
            img_back_send.at[k],
            img_back_recv.at[k],
            column_peer(k, -1),
        )
        for k in range(n_img - 1, 0, -1)
    ]

    for k, copy in enumerate(nears, 1):
        copy.wait_recv()
        near = near + near_in[k]
    far_out[...] = near
    fars = [
        send(far_out, far_in.at[k], far_send.at[k], far_recv.at[k], column_peer(k, 1))
        for k in range(1, n_img)
    ]

    own = txt_total[0:pad]
    for k, copy in zip(range(n_txt - 1, 0, -1), txt_backs):
        copy.wait_recv()
        own = own + txt_back[k].astype(jnp.float32)
    text_grad_ref[...] = own[0:rows]
    own = img_total[0:pad]
    for k, copy in zip(range(n_img - 1, 0, -1), img_backs):
        copy.wait_recv()
        own = own + img_back[k].astype(jnp.float32)
    image_grad_ref[...] = own[0:rows]

    for k, copy in enumerate(fars, 1):
        copy.wait_recv()
        near = near + far_in[k]
    sums_ref[...] = near / (rows * groups * members)
    for copy in copies:
        copy.wait_send()


def deliver(
    image_ref, text_ref, sums_ref, loss_out, image_out, text_out, temp_out, bias_out, held, sem
):
    pairs = [(image_ref, image_out), (text_ref, text_out)]
    pairs += [(held.at[i], out) for i, out in enumerate((loss_out, temp_out, bias_out))]
    copies = [pltpu.make_async_copy(src, dst, sem.at[i]) for i, (src, dst) in enumerate(pairs)]
    copies[0].start()
    copies[1].start()
    sums = sums_ref[...]
    for i in range(3):
        held[i, 0] = sums[i, 0]
        copies[2 + i].start()
    for copy in copies:
        copy.wait()


def body(groups, members, pic, pic_mul, cap, cap_mul, sharp, shift):
    rows, width = pic.shape
    pad = -(-rows // 16) * 16
    cores, chips, sides, planes = layout(groups, members)
    n_img, n_txt = planes, sides * chips * cores
    vmem = pl.BlockSpec(memory_space=pltpu.VMEM)
    hbm = pl.BlockSpec(memory_space=pltpu.HBM)
    bf16, f32, dma = jnp.bfloat16, jnp.float32, pltpu.SemaphoreType.DMA
    one = jax.ShapeDtypeStruct((1,), f32)
    grad = jax.ShapeDtypeStruct((rows, width), f32)
    tile = jax.ShapeDtypeStruct((8, 128), f32)
    image_grad, text_grad, sums = pl.pallas_call(
        functools.partial(kernel, groups, members, rows, pad),
        out_shape=(pltpu.VMEM((rows, width), f32), pltpu.VMEM((rows, width), f32), pltpu.VMEM((8, 128), f32)),
        in_specs=[hbm] * 6,
        out_specs=(vmem, vmem, vmem),
        scratch_shapes=[
            pltpu.VMEM((rows, width), bf16),
            pltpu.VMEM((rows,), f32),
            pltpu.VMEM((rows, width), bf16),
            pltpu.VMEM((rows,), f32),
            pltpu.SMEM((1,), f32),
            pltpu.SMEM((1,), f32),
            dma((6,)),
            pltpu.VMEM((pad, width), f32),
            pltpu.VMEM((n_img * pad, width), bf16),
            pltpu.VMEM((n_txt * pad, width), bf16),
            pltpu.VMEM((n_img * pad, width), bf16),
            pltpu.VMEM((n_txt * pad, width), bf16),
            pltpu.VMEM((n_img, pad, width), bf16),
            pltpu.VMEM((n_txt, pad, width), bf16),
            pltpu.VMEM((8, 128), f32),
            pltpu.VMEM((n_txt, 8, 128), f32),
            pltpu.VMEM((8, 128), f32),
            pltpu.VMEM((n_img, 8, 128), f32),
            dma((n_img,)),
            dma((n_img,)),
            dma((n_txt,)),
            dma((n_txt,)),
            dma((n_img,)),
            dma((n_img,)),
            dma((n_txt,)),
            dma((n_txt,)),
            dma((n_txt,)),
            dma((n_txt,)),
            dma((n_img,)),
            dma((n_img,)),
        ],
        compiler_params=pltpu.CompilerParams(
            collective_id=0, has_side_effects=True, vmem_limit_bytes=63 * 1024 * 1024
        ),
    )(pic, pic_mul, cap, cap_mul, sharp, shift)
    return pl.pallas_call(
        deliver,
        out_shape=(one, grad, grad, one, one),
        in_specs=[vmem] * 3,
        out_specs=(hbm, hbm, hbm, hbm, hbm),
        scratch_shapes=[pltpu.SMEM((3, 1), f32), dma((5,))],
        compiler_params=pltpu.CompilerParams(vmem_limit_bytes=4 * 1024 * 1024),
    )(image_grad, text_grad, sums)


def solution(mesh):
    placed = (
        P(("blk", "grp"), None),
        P(("blk", "grp")),
        P(("blk", "grp"), None),
        P(("blk", "grp")),
        P(),
        P(),
    )
    return jax.shard_map(
        functools.partial(body, mesh.shape["blk"], mesh.shape["grp"]),
        mesh=mesh,
        in_specs=placed,
        out_specs=(P(), P(("blk", "grp"), None), P(("blk", "grp"), None), P(), P()),
        check_vma=False,
    )
```

```python
import functools
import itertools

import jax
import jax.numpy as jnp
from jax import lax
from jax.experimental import pallas as pl
from jax.experimental.pallas import tpu as pltpu
from jax.sharding import PartitionSpec as P

MESH = pl.DeviceIdType.MESH


def layout(groups, members):
    cores = 2 if groups % 2 == 0 else 1
    sides = 2 if members % 2 == 0 else 1
    return cores, groups // cores, sides, members // sides


def kernel(
    groups,
    members,
    rows,
    pad,
    pic_hbm,
    pic_mul_hbm,
    cap_hbm,
    cap_mul_hbm,
    sharp_hbm,
    shift_hbm,
    image_grad_ref,
    text_grad_ref,
    sums_ref,
    pic_ref,
    pic_mul_ref,
    cap_ref,
    cap_mul_ref,
    sharp_ref,
    shift_ref,
    load_sem,
    stage,
    img,
    txt,
    img_part,
    txt_part,
    img_back,
    txt_back,
    near_out,
    near_in,
    far_out,
    far_in,
    img_send,
    img_recv,
    txt_send,
    txt_recv,
    img_back_send,
    img_back_recv,
    txt_back_send,
    txt_back_recv,
    near_send,
    near_recv,
    far_send,
    far_recv,
):
    cores, chips, sides, planes = layout(groups, members)
    b, g = lax.axis_index("blk"), lax.axis_index("grp")
    chip, core = b // cores, b % cores
    z, y = g // sides, g % sides
    offsets = list(itertools.product(range(sides), range(chips), range(cores)))
    n_img, n_txt = planes, len(offsets)

    def plane_peer(index, sign):
        dy, dx, dc = offsets[index]
        y2 = (y + (dy if sign > 0 else sides - dy)) % sides
        x2 = (chip + (dx if sign > 0 else chips - dx)) % chips
        c2 = (core + (dc if sign > 0 else cores - dc)) % cores
        return (x2 * cores + c2, z * sides + y2)

    def column_peer(index, sign):
        z2 = (z + (index if sign > 0 else planes - index)) % planes
        return (b, z2 * sides + y)

    barrier = pltpu.get_barrier_semaphore()
    for k in range(n_img - 1, 0, -1):
        pl.semaphore_signal(barrier, inc=1, device_id=column_peer(k, 1), device_id_type=MESH)
    for k in range(n_txt - 1, 0, -1):
        pl.semaphore_signal(barrier, inc=1, device_id=plane_peer(k, 1), device_id_type=MESH)

    loads = [
        pltpu.make_async_copy(src, dst, load_sem.at[i])
        for i, (src, dst) in enumerate(
            [
                (pic_mul_hbm, pic_mul_ref),
                (pic_hbm, pic_ref),
                (cap_mul_hbm, cap_mul_ref),
                (cap_hbm, cap_ref),
                (sharp_hbm, sharp_ref),
                (shift_hbm, shift_ref),
            ]
        )
    ]
    for load in loads:
        load.start()
    def decode(codes_ref, mul_ref, slot):
        diagonal = lax.broadcasted_iota(jnp.int32, (rows, rows), 0) == lax.broadcasted_iota(
            jnp.int32, (rows, rows), 1
        )
        across = jnp.broadcast_to(mul_ref[...].reshape(1, rows), (rows, rows))
        scale = jnp.sum(jnp.where(diagonal, across, 0.0), axis=1, keepdims=True)
        stage[0:rows, :] = scale * codes_ref[...].astype(jnp.float32)
        slot[0:pad, :] = stage[...].astype(jnp.bfloat16)

    def block(ref, k):
        return ref.at[pl.ds(k * pad, pad), :]

    stage[...] = jnp.zeros_like(stage)
    loads[0].wait()
    loads[1].wait()
    decode(pic_ref, pic_mul_ref, img)
    pl.semaphore_wait(barrier, n_img - 1 + n_txt - 1)

    copies = []

    def send(src, dst, send_sem, recv_sem, peer):
        copy = pltpu.make_async_remote_copy(
            src_ref=src,
            dst_ref=dst,
            send_sem=send_sem,
            recv_sem=recv_sem,
            device_id=peer,
            device_id_type=MESH,
        )
        copy.start()
        copies.append(copy)
        return copy

    gathers = [
        send(block(img, 0), block(img, k), img_send.at[k], img_recv.at[k], column_peer(k, 1))
        for k in range(n_img - 1, 0, -1)
    ]
    loads[2].wait()
    loads[3].wait()
    decode(cap_ref, cap_mul_ref, txt)
    direct = [k for k in range(n_txt - 1, 0, -1) if k % cores == 0] + list(range(cores - 1, 0, -1))
    arrivals = {}
    for k in direct:
        arrivals[k] = send(
            block(txt, 0), block(txt, k), txt_send.at[k], txt_recv.at[k], plane_peer(k, 1)
        )
    loads[4].wait()
    loads[5].wait()
    for k in sorted(arrivals, key=lambda k: offsets[k][0] + (offsets[k][1] > 0)):
        arrivals[k].wait_recv()
        if k >= cores:
            for c in range(1, cores):
                gathers.append(
                    send(
                        block(txt, k),
                        block(txt, k + c),
                        txt_send.at[k + c],
                        txt_recv.at[k + c],
                        plane_peer(c, 1),
                    )
                )
    for copy in gathers:
        copy.wait_recv()

    sharp = sharp_ref[0]
    shift = shift_ref[0]
    images, texts = img[...], txt[...]
    dots = lax.dot_general(
        images, texts, (((1,), (1,)), ((), ())), preferred_element_type=jnp.float32
    )
    logits = sharp * dots + shift
    row = lax.broadcasted_iota(jnp.int32, dots.shape, 0)
    col = lax.broadcasted_iota(jnp.int32, dots.shape, 1)
    positive = (row == col) & (row < pad)
    real = (row % pad < rows) & (col % pad < rows)
    small = jnp.exp(-jnp.abs(logits))
    below = 1.0 / (1.0 + small)
    slopes = jnp.where(logits >= 0, below, small * below) - jnp.where(positive, 1.0, 0.0)
    terms = jnp.maximum(jnp.where(positive, -logits, logits), 0.0) + jnp.log1p(small)
    weights = (sharp * slopes).astype(jnp.bfloat16)

    def total(x):
        return jnp.sum(jnp.sum(x, axis=0, keepdims=True), axis=1, keepdims=True)

    lane = lax.broadcasted_iota(jnp.int32, near_out.shape, 0)
    near = jnp.where(
        lane == 0,
        total(jnp.where(real, terms, 0.0)),
        jnp.where(lane == 1, total(slopes * dots), total(jnp.where(real, slopes, 0.0))),
    )
    near_out[...] = near
    nears = [
        send(near_out, near_in.at[k], near_send.at[k], near_recv.at[k], plane_peer(k, 1))
        for k in range(1, n_txt)
    ]

    txt_backs = []
    half = (n_txt // 2) * pad
    for low, high in ((half, n_txt * pad), (0, half)):
        txt_total = lax.dot_general(
            weights[:, low:high], images, (((0,), (0,)), ((), ())), preferred_element_type=jnp.float32
        )
        txt_part[low:high, :] = txt_total.astype(jnp.bfloat16)
        for k in range(high // pad - 1, max(low // pad, 1) - 1, -1):
            txt_backs.append(
                send(
                    block(txt_part, k),
                    txt_back.at[k],
                    txt_back_send.at[k],
                    txt_back_recv.at[k],
                    plane_peer(k, -1),
                )
            )
    img_total = jnp.dot(weights, texts, preferred_element_type=jnp.float32)
    img_part[...] = img_total.astype(jnp.bfloat16)
    img_backs = [
        send(
            block(img_part, k),
            img_back.at[k],
            img_back_send.at[k],
            img_back_recv.at[k],
            column_peer(k, -1),
        )
        for k in range(n_img - 1, 0, -1)
    ]

    for k, copy in enumerate(nears, 1):
        copy.wait_recv()
        near = near + near_in[k]
    far_out[...] = near
    fars = [
        send(far_out, far_in.at[k], far_send.at[k], far_recv.at[k], column_peer(k, 1))
        for k in range(1, n_img)
    ]

    own = txt_total[0:pad]
    for k, copy in zip(range(n_txt - 1, 0, -1), txt_backs):
        copy.wait_recv()
        own = own + txt_back[k].astype(jnp.float32)
    text_grad_ref[...] = own[0:rows]
    own = img_total[0:pad]
    for k, copy in zip(range(n_img - 1, 0, -1), img_backs):
        copy.wait_recv()
        own = own + img_back[k].astype(jnp.float32)
    image_grad_ref[...] = own[0:rows]

    for k, copy in enumerate(fars, 1):
        copy.wait_recv()
        near = near + far_in[k]
    sums_ref[...] = near / (rows * groups * members)
    for copy in copies:
        copy.wait_send()


def deliver(
    image_ref, text_ref, sums_ref, loss_out, image_out, text_out, temp_out, bias_out, held, sem
):
    pairs = [(image_ref, image_out), (text_ref, text_out)]
    pairs += [(held.at[i], out) for i, out in enumerate((loss_out, temp_out, bias_out))]
    copies = [pltpu.make_async_copy(src, dst, sem.at[i]) for i, (src, dst) in enumerate(pairs)]
    copies[0].start()
    copies[1].start()
    sums = sums_ref[...]
    for i in range(3):
        held[i, 0] = sums[i, 0]
        copies[2 + i].start()
    for copy in copies:
        copy.wait()


def body(groups, members, pic, pic_mul, cap, cap_mul, sharp, shift):
    rows, width = pic.shape
    pad = -(-rows // 16) * 16
    cores, chips, sides, planes = layout(groups, members)
    n_img, n_txt = planes, sides * chips * cores
    vmem = pl.BlockSpec(memory_space=pltpu.VMEM)
    hbm = pl.BlockSpec(memory_space=pltpu.HBM)
    bf16, f32, dma = jnp.bfloat16, jnp.float32, pltpu.SemaphoreType.DMA
    one = jax.ShapeDtypeStruct((1,), f32)
    grad = jax.ShapeDtypeStruct((rows, width), f32)
    tile = jax.ShapeDtypeStruct((8, 128), f32)
    image_grad, text_grad, sums = pl.pallas_call(
        functools.partial(kernel, groups, members, rows, pad),
        out_shape=(pltpu.VMEM((rows, width), f32), pltpu.VMEM((rows, width), f32), pltpu.VMEM((8, 128), f32)),
        in_specs=[hbm] * 6,
        out_specs=(vmem, vmem, vmem),
        scratch_shapes=[
            pltpu.VMEM((rows, width), bf16),
            pltpu.VMEM((rows,), f32),
            pltpu.VMEM((rows, width), bf16),
            pltpu.VMEM((rows,), f32),
            pltpu.SMEM((1,), f32),
            pltpu.SMEM((1,), f32),
            dma((6,)),
            pltpu.VMEM((pad, width), f32),
            pltpu.VMEM((n_img * pad, width), bf16),
            pltpu.VMEM((n_txt * pad, width), bf16),
            pltpu.VMEM((n_img * pad, width), bf16),
            pltpu.VMEM((n_txt * pad, width), bf16),
            pltpu.VMEM((n_img, pad, width), bf16),
            pltpu.VMEM((n_txt, pad, width), bf16),
            pltpu.VMEM((8, 128), f32),
            pltpu.VMEM((n_txt, 8, 128), f32),
            pltpu.VMEM((8, 128), f32),
            pltpu.VMEM((n_img, 8, 128), f32),
            dma((n_img,)),
            dma((n_img,)),
            dma((n_txt,)),
            dma((n_txt,)),
            dma((n_img,)),
            dma((n_img,)),
            dma((n_txt,)),
            dma((n_txt,)),
            dma((n_txt,)),
            dma((n_txt,)),
            dma((n_img,)),
            dma((n_img,)),
        ],
        compiler_params=pltpu.CompilerParams(
            collective_id=0, has_side_effects=True, vmem_limit_bytes=63 * 1024 * 1024
        ),
    )(pic, pic_mul, cap, cap_mul, sharp, shift)
    return pl.pallas_call(
        deliver,
        out_shape=(one, grad, grad, one, one),
        in_specs=[vmem] * 3,
        out_specs=(hbm, hbm, hbm, hbm, hbm),
        scratch_shapes=[pltpu.SMEM((3, 1), f32), dma((5,))],
        compiler_params=pltpu.CompilerParams(vmem_limit_bytes=4 * 1024 * 1024),
    )(image_grad, text_grad, sums)


def solution(mesh):
    placed = (
        P(("blk", "grp"), None),
        P(("blk", "grp")),
        P(("blk", "grp"), None),
        P(("blk", "grp")),
        P(),
        P(),
    )
    return jax.shard_map(
        functools.partial(body, mesh.shape["blk"], mesh.shape["grp"]),
        mesh=mesh,
        in_specs=placed,
        out_specs=(P(), P(("blk", "grp"), None), P(("blk", "grp"), None), P(), P()),
        check_vma=False,
    )
```
